256 devices in a mesh: curve: 64 (over y, z, core), band: 4 (over x).
Axes of the slice: x: 4, y: 4, z: 8, core: 2. Of those that a mesh axis runs over, the one named last changes fastest.
Arguments:
- state: float32 [16, 16384, 128], P('band', 'curve'), may hold values from -3 to 3
- blocks: bfloat16 [16384, 4, 128, 128], P('curve', 'band'), may hold values from -0.25 to 0.25
- diag_blocks: bfloat16 [16384, 128, 128], P(('curve', 'band')), may hold values from -1 to 1, as said below
- block_cols: int32 [16384, 4], P('curve', 'band'), may hold values from 0 to 16383, as said below
Outputs:
- updated: float32 [16, 16384, 128], P('band', 'curve')
The draws below stay inside these ranges and needn't reach their ends.
Inputs may be any that keep to these rules, and one draw needn't show every extreme that they name: `diag_blocks`: every diagonal block is symmetric. `block_cols`: A column is never the row's own patch, and no pair of patches is stored twice, in either order. The owner of patch p is index p // 256 of curve. Of the 256 rows of one index of curve, in each slot exactly 64 have their column on another index: 2 on each of 32 other indices; the columns of the others lie on the own index.
All inputs are finite; a program needn't handle non-finite values.
Results may differ from the reference program's by a relative error of at most 0.0003.
The reference program's roundings to bfloat16 on the way count: a program that leaves them out, or rounds other values in their place, can miss the bound.
Values may be sent and summed in bfloat16 or wider, within the bound.
A program may use at most 64 MiB of HBM per device.

```python
import jax
import jax.numpy as jnp
from jax import lax

BS = 128
NV = 16
P_DEV = 256
CAP = 2
TAYLOR = 16
SLOTS = 4
PATCHES = 16384
REMOTE = 64


def draw_state(key, part):
    key_base, key_rows, key_cols = jax.random.split(key, 3)
    patch_index = jnp.arange(PATCHES, dtype=jnp.float32)
    ramp = (1.0 + 2.0 * patch_index / (PATCHES - 1.0)) / 3.0
    row_scale = 10.0 ** jax.random.uniform(key_rows, (PATCHES,), minval=-1.0, maxval=0.0)
    col_scale = 10.0 ** jax.random.uniform(key_cols, (NV,), minval=-0.92, maxval=0.08)
    base = jnp.clip(jax.random.normal(key_base, (NV, PATCHES, BS)), -2.5, 2.5)
    return base * col_scale[:, None, None] * (row_scale * ramp)[None, :, None]


def draw_diag_blocks(key, part):
    raw = jax.random.normal(key, (PATCHES, BS, BS))
    symmetric = (raw + jnp.swapaxes(raw, 1, 2)) * 0.5 ** 0.5 / (5.0 * BS) ** 0.5
    identity = jnp.eye(BS, dtype=jnp.float32)
    return (symmetric - 0.3 * identity[None, :, :]).astype(jnp.bfloat16)


def column_list(key, device, slot_id):
    devices = PATCHES // P_DEV
    mixed = jax.random.fold_in(jax.random.fold_in(jax.random.fold_in(key, 7331), device), slot_id)
    key_order, key_peer, key_gap = jax.random.split(mixed, 3)
    order = jax.random.permutation(key_order, P_DEV)
    place = jnp.zeros((P_DEV,), jnp.int32).at[order].set(jnp.arange(P_DEV, dtype=jnp.int32))
    offsets = 1 + jax.random.permutation(key_peer, devices - 1)
    group_index = jnp.minimum(place // CAP, devices // 2 - 1)
    device_shift = jnp.where(place < REMOTE, offsets[group_index], 0)
    range_width = P_DEV // (2 * SLOTS)
    gap = 1 + slot_id * range_width + jax.random.randint(key_gap, (P_DEV,), 0, range_width - 1)
    row_index = jnp.arange(P_DEV, dtype=jnp.int32)
    return (device + device_shift) % devices * P_DEV + (row_index + gap) % P_DEV


def draw_block_cols(key, part):
    devices = PATCHES // P_DEV
    device_ids = jnp.arange(devices, dtype=jnp.int32)
    slot_ids = jnp.arange(SLOTS, dtype=jnp.int32)
    table = jax.vmap(lambda device: jax.vmap(lambda slot_id: column_list(key, device, slot_id))(slot_ids))(device_ids)
    return jnp.transpose(table, (0, 2, 1)).reshape(PATCHES, SLOTS).astype(jnp.int32)


def levels(stream_key, dims, pieces, least, largest):
    def one(position, parts):
        heights = jax.random.uniform(jax.random.fold_in(jax.random.fold_in(stream_key, 6), position), (parts,), jnp.float32, least / len(pieces), largest / len(pieces))
        return jnp.repeat(jnp.exp(heights), dims[position] // parts).reshape((-1,) + (1,) * (len(dims) - position - 1))

    gain = one(*pieces[0])
    for cut in pieces[1:]:
        gain = gain * one(*cut)
    return gain


def bell_draw(own_key, extent, spread, most, pieces=(), kind=jnp.bfloat16):
    factor_of = levels(own_key, extent, pieces, -0.22, 0.18) if pieces else 1.0
    entries = jax.random.normal(own_key, extent, jnp.float32) * spread * factor_of
    return jnp.minimum(jnp.maximum(entries, -most), most).astype(kind)


def setup_inputs(seed: int = 0) -> dict:
    seeds = jax.random.split(jax.random.key(seed), 5)
    return {
        "state": draw_state(jax.random.fold_in(seeds[4], 71), 0),
        "blocks": bell_draw(seeds[1], (PATCHES, SLOTS, BS, BS), (5 * BS) ** -0.5, 0.25, ((0, 64), (1, 4))),
        "diag_blocks": draw_diag_blocks(jax.random.fold_in(seeds[4], 71), 0),
        "block_cols": draw_block_cols(jax.random.fold_in(seeds[4], 71), 0),
    }


epsilon = 1e-06
time_step = 0.5
quadratic = 1.0

def nonlinear(field):
    return quadratic * field * field - field * field * field

def phi_weights(alpha_first, beta_first, alpha_second):

    def advance(turn, carry):
        term_one, term_two, total_one, total_two = carry
        factor = time_step / (turn + 1.0)
        next_one = factor * (alpha_first * term_one + beta_first * term_two)
        next_two = factor * (beta_first * term_one + alpha_second * term_two)
        return (next_one, next_two, total_one + next_one, total_two + next_two)
    ones = jnp.ones_like(alpha_first)
    zeros = jnp.zeros_like(alpha_first)
    result = lax.fori_loop(1, TAYLOR, advance, (ones, zeros, ones, zeros))
    return (result[2], result[3])

def apply_operator(vector, blocks, diag_blocks, block_cols):
    vectors, patches, node_count = vector.shape
    slot_count = blocks.shape[1]
    group = P_DEV
    count = patches // group
    columns = block_cols.reshape(-1)
    column_field = vector[:, columns, :].reshape(vectors, count, group, slot_count, node_count)
    column_field = jnp.transpose(column_field, (1, 0, 2, 3, 4))
    row_field = jnp.transpose(vector.reshape(vectors, count, group, node_count), (1, 0, 2, 3))
    stored = blocks.reshape(count, group, slot_count, node_count, node_count)
    diagonal = diag_blocks.reshape(count, group, node_count, node_count)

    def piece(operands):
        stored_part, diagonal_part, row_part, column_part = operands
        stored_part = stored_part.astype(jnp.float32)
        diagonal_part = diagonal_part.astype(jnp.float32)
        row_part = row_part.astype(jnp.float32)
        column_part = column_part.astype(jnp.float32)
        forward = jnp.einsum('rbac,vrbc->vra', stored_part, column_part)
        forward = forward + jnp.einsum('rac,vrc->vra', diagonal_part, row_part)
        mirrored = jnp.einsum('rbac,vra->vrbc', stored_part, row_part)
        return (forward, mirrored)
    forward, mirrored = lax.map(piece, (stored, diagonal, row_field, column_field))
    forward = jnp.transpose(forward, (1, 0, 2, 3)).reshape(vectors, patches, node_count)
    mirrored = jnp.transpose(mirrored, (1, 0, 2, 3, 4)).reshape(vectors, patches * slot_count, node_count)
    return forward.at[:, columns, :].add(mirrored)

def reference(state, blocks, diag_blocks, block_cols):
    linear = apply_operator(state.astype(jnp.bfloat16), blocks, diag_blocks, block_cols)
    drive = linear + nonlinear(state)
    beta_zero = jnp.sqrt(lax.optimization_barrier(jnp.sum(drive * drive, axis=(1, 2))) + epsilon)
    first = drive / beta_zero[:, None, None]
    image = apply_operator(first.astype(jnp.bfloat16), blocks, diag_blocks, block_cols)
    alpha_first = lax.optimization_barrier(jnp.sum(first * image, axis=(1, 2)))
    rest = image - alpha_first[:, None, None] * first
    beta_first = jnp.sqrt(lax.optimization_barrier(jnp.sum(rest * rest, axis=(1, 2))) + epsilon)
    second = rest / beta_first[:, None, None]
    image_second = apply_operator(second.astype(jnp.bfloat16), blocks, diag_blocks, block_cols)
    image_second = image_second - beta_first[:, None, None] * first
    alpha_second = lax.optimization_barrier(jnp.sum(second * image_second, axis=(1, 2)))
    weight_one, weight_two = phi_weights(alpha_first, beta_first, alpha_second)
    combined = weight_one[:, None, None] * first + weight_two[:, None, None] * second
    return state + time_step * beta_zero[:, None, None] * combined
```

```python
import functools

import jax
import jax.numpy as jnp
from jax import lax
from jax.experimental import pallas as pl
from jax.experimental.pallas import tpu as pltpu
from jax.sharding import PartitionSpec as P

CAP = 2
TAYLOR = 16
APPS = 3
GROUPS = 4

epsilon = 1e-06
time_step = 0.5
quadratic = 1.0

F32 = jnp.float32
BF16 = jnp.bfloat16


def phi_weights(alpha_first, beta_first, alpha_second):
    term_one = jnp.ones_like(alpha_first)
    term_two = jnp.zeros_like(alpha_first)
    total_one, total_two = term_one, term_two
    for turn in range(1, TAYLOR):
        factor = time_step / (turn + 1.0)
        next_one = factor * (alpha_first * term_one + beta_first * term_two)
        next_two = factor * (beta_first * term_one + alpha_second * term_two)
        term_one, term_two = next_one, next_two
        total_one, total_two = total_one + next_one, total_two + next_two
    return total_one, total_two


def kernel(
    curve,
    state_ref,
    col_ref,
    row_ref,
    blocks_hbm,
    diag_hbm,
    out_ref,
    blocks,
    diag,
    slabs,
    staging,
    pool,
    outbox,
    inbox,
    mirrored,
    forward,
    ret_out,
    ret_in,
    share,
    relay_in,
    sum_in,
    first,
    rest,
    onehot,
    ask_out,
    ask_in,
    index_vmem,
    index_smem,
    quad,
    band_in,
    total_out,
    total_in,
    load_sem,
    ask_sem,
    index_sem,
    slab_send,
    slab_recv,
    gather_sem,
    return_sem,
    sum_send,
    sum_recv,
    band_sem,
    total_sem,
):
    per, rows, nodes = state_ref.shape
    vectors = per * GROUPS
    half = per // 2
    slots = curve * CAP
    quarter = diag.shape[0]
    me = lax.axis_index("curve")
    band = lax.axis_index("band")
    shift = rows.bit_length() - 1

    def other(step):
        return lax.rem(band + step, GROUPS)

    def peer(step):
        return lax.rem(me + step, curve)

    def load(chunk_ref, buffer, n):
        return pltpu.make_async_copy(chunk_ref, buffer, load_sem.at[n])

    load(blocks_hbm, blocks, 0).start()
    load(diag_hbm, diag, 1).start()

    barrier = pltpu.get_barrier_semaphore()

    @pl.loop(1, curve)
    def _(step):
        pl.semaphore_signal(barrier, inc=1, device_id={"curve": peer(step)})

    for step in range(1, GROUPS):
        pl.semaphore_signal(barrier, inc=1, device_id={"band": other(step)})

    own_col = lax.shift_right_logical(col_ref[...], shift)
    own_row = lax.shift_right_logical(row_ref[...], shift)
    tgt_row = row_ref[...] & (rows - 1)
    remote_row = own_row != me
    sub = lax.broadcasted_iota(jnp.int32, (rows, rows), 0)
    lane = lax.broadcasted_iota(jnp.int32, (rows, rows), 1)
    same = own_col == own_row
    rank_row = jnp.sum((same & (sub < lane)).astype(jnp.int32), axis=0, keepdims=True)
    rank_col = jnp.sum((same & (lane < sub)).astype(jnp.int32), axis=1, keepdims=True)
    bucket_col = jnp.where(own_col != me, own_col * CAP + rank_col, -1)
    pick_row = jnp.where(remote_row, rows + own_row * CAP + rank_row, tgt_row)
    padded = jnp.where(remote_row, own_row * 8 + rank_row, -1)
    place = lax.broadcasted_iota(jnp.int32, (curve * 8, rows), 0)
    wanted = jnp.sum(jnp.where(place == padded, tgt_row + 1, 0), axis=1, keepdims=True)
    ask_out[...] = jnp.broadcast_to(wanted, ask_out.shape)
    ask_in[pl.ds(pl.multiple_of(me * 8, 8), 8), :] = jnp.zeros((8, ask_in.shape[1]), jnp.int32)
    lane_slot = lax.broadcasted_iota(jnp.int32, (rows, slots), 1)
    source = lax.broadcasted_iota(jnp.int32, (rows, slots), 0)
    row_of = jnp.sum(jnp.where(bucket_col == lane_slot, source, 0), axis=0, keepdims=True)
    index_vmem[0:1, 0:rows] = jnp.clip(pick_row, 0, rows + slots - 1)
    index_vmem[1:2, 0:slots] = jnp.clip(row_of, 0, rows - 1)
    onehot[:, 0:rows] = ((tgt_row == sub) & ~remote_row).astype(F32).astype(BF16)

    pl.semaphore_wait(barrier, curve - 1 + GROUPS - 1)

    def ask_copy(target, own):
        return pltpu.make_async_remote_copy(
            src_ref=ask_out.at[pl.ds(pl.multiple_of(target * 8, 8), 8)],
            dst_ref=ask_in.at[pl.ds(pl.multiple_of(own * 8, 8), 8)],
            send_sem=ask_sem.at[0],
            recv_sem=ask_sem.at[1],
            device_id={"curve": target},
        )

    @pl.loop(1, curve)
    def _(step):
        ask_copy(peer(step), me).start()

    def wait_all(buffer, size, send, recv, wait_send):
        view = buffer.at[pl.ds(0, (curve - 1) * size)]
        copy = pltpu.make_async_remote_copy(
            src_ref=view, dst_ref=view, send_sem=send, recv_sem=recv, device_id={"curve": peer(1)}
        )
        if wait_send:
            copy.wait_send()
        else:
            copy.wait_recv()

    def take_asked():
        wait_all(ask_in, 8, ask_sem.at[0], ask_sem.at[1], False)
        place = lax.broadcasted_iota(jnp.int32, (curve * 8, slots), 0)
        slot = lax.broadcasted_iota(jnp.int32, (curve * 8, slots), 1)
        chosen = place == lax.shift_right_logical(slot, 1) * 8 + (slot & 1)
        asked = jnp.sum(jnp.where(chosen, ask_in[:, 0:slots], 0), axis=0, keepdims=True)
        index_vmem[2:3, 0:slots] = jnp.clip(asked - 1, 0, rows - 1)
        sub = lax.broadcasted_iota(jnp.int32, (rows, slots), 0)
        onehot[:, rows:] = (asked - 1 == sub).astype(F32).astype(BF16)
        copy = pltpu.make_async_copy(index_vmem, index_smem, index_sem)
        copy.start()
        copy.wait()
        wait_all(ask_out, 8, ask_sem.at[0], ask_sem.at[1], True)

    def slab_copy(app, src, dst, planes, step, n):
        return pltpu.make_async_remote_copy(
            src_ref=slabs.at[app, src, planes],
            dst_ref=slabs.at[app, dst, planes],
            send_sem=slab_send.at[app, n],
            recv_sem=slab_recv.at[app, n],
            device_id={"band": other(step)},
        )

    def interleave(app, group):
        for t in range(per):
            v = group * per + t
            staging[pl.ds(v, rows, stride=vectors), :] = slabs[app, group, t].astype(F32)

    low, high, every = pl.ds(0, half), pl.ds(half, half), pl.ds(0, per)

    def exchange_band(app, field):
        for t in range(per):
            slabs[app, 0, t] = field[t].astype(BF16)
        right = slab_copy(app, 0, 3, every, 1, 0)
        left = slab_copy(app, 0, 1, every, GROUPS - 1, 1)
        right.start()
        left.start()
        interleave(app, 0)
        right.wait_recv()
        on_right = slab_copy(app, 3, 2, low, 1, 2)
        on_right.start()
        left.wait_recv()
        on_left = slab_copy(app, 1, 2, high, GROUPS - 1, 3)
        on_left.start()
        interleave(app, 3)
        interleave(app, 1)
        on_right.wait_recv()
        on_left.wait_recv()
        interleave(app, 2)
        for copy in (right, left, on_right, on_left):
            copy.wait_send()

        @pl.loop(0, rows // 16)
        def _(n):
            piece = pl.ds(pl.multiple_of(n * 16 * vectors, 256), 16 * vectors)
            pool[pl.ds(pl.multiple_of(n * 16, 16), 16)] = (
                staging[piece, :].astype(BF16).reshape(16, vectors, nodes)
            )

    def tile(n):
        return pl.ds(pl.multiple_of(n * vectors, 16), vectors)

    wide = CAP * vectors

    def send_gather(app):
        @pl.loop(1, curve)
        def _(step):
            target = peer(step)
            for k in range(CAP):
                n = target * CAP + k
                outbox[tile(n), :] = pool[index_smem[2, n]]
            pltpu.make_async_remote_copy(
                src_ref=outbox.at[pl.ds(pl.multiple_of(target * wide, wide), wide)],
                dst_ref=inbox.at[app, pl.ds(pl.multiple_of(me * wide, wide), wide)],
                send_sem=gather_sem.at[app, 0],
                recv_sem=gather_sem.at[app, 1],
                device_id={"curve": target},
            ).start()

    def take_gather(app):
        wait_all(inbox.at[app], wide, gather_sem.at[app, 0], gather_sem.at[app, 1], False)

        @pl.loop(0, slots // 8)
        def _(n):
            piece = pl.ds(pl.multiple_of(n * 8 * vectors, 128), 8 * vectors)
            pool[pl.ds(rows + n * 8, 8)] = inbox[app, piece, :].reshape(8, vectors, nodes)

        wait_all(outbox, wide, gather_sem.at[app, 0], gather_sem.at[app, 1], True)

    def mirror():
        @pl.loop(0, rows, unroll=8)
        def _(r):
            mirrored[tile(r), :] = jnp.dot(pool[r], blocks[r], preferred_element_type=F32)

    def send_return(app):
        mine = pl.ds(pl.multiple_of(me * wide, wide), wide)
        ret_in[app, mine, :] = jnp.zeros((wide, nodes), F32)

        @pl.loop(1, curve)
        def _(step):
            target = peer(step)
            for k in range(CAP):
                n = target * CAP + k
                r = index_smem[1, n]
                ret_out[tile(n), :] = jnp.dot(pool[r], blocks[r], preferred_element_type=F32)
            pltpu.make_async_remote_copy(
                src_ref=ret_out.at[pl.ds(pl.multiple_of(target * wide, wide), wide)],
                dst_ref=ret_in.at[app, mine],
                send_sem=return_sem.at[app, 0],
                recv_sem=return_sem.at[app, 1],
                device_id={"curve": target},
            ).start()

    def contract(left, right):
        return lax.dot_general(left, right, (((1,), (1,)), ((), ())), preferred_element_type=F32)

    def multiply_forward(app):
        zeros = jnp.zeros((vectors, nodes), F32)

        def one(r, total):
            product = contract(pool[index_smem[0, r]], blocks[r])
            if app < APPS - 1:
                forward[tile(r), :] = product
            if app > 0:
                total = total + product * pool[r].astype(F32)
            return total

        total = lax.fori_loop(0, rows, one, zeros, unroll=8)

        def two(q, total):
            r = band * quarter + q
            left = pool[r]
            product = contract(left, diag[q])
            if app < APPS - 1:
                forward[tile(r), :] += product
            if app > 0:
                total = total + product * left.astype(F32)
            return total

        return lax.fori_loop(0, quarter, two, 2.0 * total, unroll=8)

    def split(value):
        upper = value.astype(BF16)
        return upper, (value - upper.astype(F32)).astype(BF16)

    def add_up(app, group, t):
        v = group * per + t
        total = forward[pl.ds(v, rows, stride=vectors), :]
        for part in split(mirrored[pl.ds(v, rows, stride=vectors), :]):
            total += jnp.dot(onehot[:, 0:rows], part, preferred_element_type=F32)
        for part in split(ret_in[app, pl.ds(v, slots, stride=vectors), :]):
            total += jnp.dot(onehot[:, rows:], part, preferred_element_type=F32)
        share[group, t] = total

    def sum_copy(app, src, dst, step, n):
        return pltpu.make_async_remote_copy(
            src_ref=src,
            dst_ref=dst,
            send_sem=sum_send.at[app, n],
            recv_sem=sum_recv.at[app, n],
            device_id={"band": other(step)},
        )

    def reduce_band(app):
        wait_all(ret_in.at[app], wide, return_sem.at[app, 0], return_sem.at[app, 1], False)
        up, down = 1, GROUPS - 1
        for t in range(half):
            add_up(app, 2, t)
        relay_up = sum_copy(app, share.at[2, low], relay_in.at[app, 0], up, 0)
        relay_up.start()
        for t in range(half, per):
            add_up(app, 2, t)
        relay_down = sum_copy(app, share.at[2, high], relay_in.at[app, 1], down, 1)
        relay_down.start()
        for t in range(half, per):
            add_up(app, 1, t)
        direct_up = sum_copy(app, share.at[1, high], sum_in.at[app, 0, high], up, 2)
        direct_up.start()
        for t in range(half):
            add_up(app, 3, t)
        direct_down = sum_copy(app, share.at[3, low], sum_in.at[app, 1, low], down, 3)
        direct_down.start()
        for t in range(half):
            add_up(app, 1, t)
        relay_up.wait_recv()
        share[1, 0:half] += relay_in[app, 0]
        last_up = sum_copy(app, share.at[1, low], sum_in.at[app, 0, low], up, 4)
        last_up.start()
        for t in range(half, per):
            add_up(app, 3, t)
        relay_down.wait_recv()
        share[3, half:per] += relay_in[app, 1]
        last_down = sum_copy(app, share.at[3, high], sum_in.at[app, 1, high], down, 5)
        last_down.start()
        for t in range(per):
            add_up(app, 0, t)
        copies = (relay_up, relay_down, direct_up, direct_down, last_up, last_down)
        for copy in copies[2:]:
            copy.wait_recv()
        for t in range(per):
            share[0, t] = share[0, t] + (sum_in[app, 0, t] + sum_in[app, 1, t])
        for copy in copies:
            copy.wait_send()
        wait_all(ret_out, wide, return_sem.at[app, 0], return_sem.at[app, 1], True)

    def send_quad(n, total):
        quad[...] = jnp.zeros_like(quad)
        for group in range(GROUPS):
            quad[group, 0:per, :] = total[group * per : (group + 1) * per, :]
        for step in range(1, GROUPS):
            pltpu.make_async_remote_copy(
                src_ref=quad.at[step],
                dst_ref=band_in.at[n, step],
                send_sem=band_sem.at[n, 0, step],
                recv_sem=band_sem.at[n, 1, step],
                device_id={"band": other(step)},
            ).start()

    def take_quad(n):
        total = quad[0]
        for step in range(1, GROUPS):
            copy = pltpu.make_async_remote_copy(
                src_ref=quad.at[step],
                dst_ref=band_in.at[n, step],
                send_sem=band_sem.at[n, 0, step],
                recv_sem=band_sem.at[n, 1, step],
                device_id={"band": other(step)},
            )
            copy.wait_recv()
            total = total + band_in[n, step]
            copy.wait_send()
        return total[0:per]

    def send_total(n, parts):
        total_out[n] = jnp.zeros_like(total_out[n])
        for k, part in enumerate(parts):
            total_out[n, k * per : (k + 1) * per, :] = part
        mine = pl.ds(pl.multiple_of(me * 16, 16), 16)
        total_in[n, mine, :] = total_out[n]

        @pl.loop(1, curve)
        def _(step):
            pltpu.make_async_remote_copy(
                src_ref=total_out.at[n],
                dst_ref=total_in.at[n, mine],
                send_sem=total_sem.at[n, 0],
                recv_sem=total_sem.at[n, 1],
                device_id={"curve": peer(step)},
            ).start()

    def take_total(n):
        wait_all(total_in.at[n], 16, total_sem.at[n, 0], total_sem.at[n, 1], False)
        total = jnp.sum(total_in[n].reshape(curve, 16, nodes), axis=0)
        wait_all(total_in.at[n], 16, total_sem.at[n, 0], total_sem.at[n, 1], True)
        total = jnp.broadcast_to(jnp.sum(total, axis=1, keepdims=True), total.shape)
        return [total[k * per : (k + 1) * per] for k in range(4)]

    def over_rows(values):
        return jnp.concatenate([jnp.sum(value, axis=0, keepdims=True) for value in values], axis=0)

    exchange_band(0, state_ref)
    take_asked()
    send_gather(0)
    load(blocks_hbm, blocks, 0).wait()
    send_return(0)
    mirror()
    load(diag_hbm, diag, 1).wait()
    take_gather(0)
    multiply_forward(0)
    reduce_band(0)
    norms = []
    for t in range(per):
        field = state_ref[t]
        drive = share[0, t] + (quadratic * field * field - field * field * field)
        first[t] = drive
        norms.append(drive * drive)
    send_total(0, [over_rows(norms)])
    norm_zero = take_total(0)[0]
    beta_zero = jnp.sqrt(norm_zero + epsilon)
    for t in range(per):
        first[t] = first[t] / beta_zero[t : t + 1]

    exchange_band(1, first)
    send_gather(1)
    send_return(1)
    mirror()
    take_gather(1)
    send_quad(0, multiply_forward(1))
    send_total(1, [take_quad(0)])
    reduce_band(1)
    alpha_first = take_total(1)[0]
    norms, along = [], []
    for t in range(per):
        value = share[0, t] - alpha_first[t : t + 1] * first[t]
        rest[t] = value
        norms.append(value * value)
        along.append(value * first[t])
    rest_norm = over_rows(norms)
    rest_along = over_rows(along)
    exchange_band(2, rest)
    send_gather(2)
    take_gather(2)
    send_quad(1, multiply_forward(2))
    send_total(2, [rest_norm, rest_along, take_quad(1)])
    norm, dot, form, _ = take_total(2)
    squared = norm + epsilon
    beta_first = jnp.sqrt(squared)
    alpha_second = form / squared - dot
    weight_one, weight_two = phi_weights(alpha_first, beta_first, alpha_second)
    scale_one = time_step * beta_zero * weight_one
    scale_two = time_step * beta_zero * weight_two / beta_first
    for t in range(per):
        out_ref[t] = state_ref[t] + (
            scale_one[t : t + 1] * first[t] + scale_two[t : t + 1] * rest[t]
        )


def body(state, blocks, diag_blocks, block_cols):
    per, rows, nodes = state.shape
    curve = lax.axis_size("curve")
    vectors = per * GROUPS
    slots = curve * CAP
    half = per // 2
    quarter = diag_blocks.shape[0]
    dma = pltpu.SemaphoreType.DMA
    vmem = pl.BlockSpec(memory_space=pltpu.VMEM)
    anywhere = pl.BlockSpec(memory_space=pl.ANY)
    return pl.pallas_call(
        functools.partial(kernel, curve),
        out_shape=jax.ShapeDtypeStruct(state.shape, F32),
        in_specs=[vmem, vmem, vmem, anywhere, anywhere],
        out_specs=vmem,
        scratch_shapes=[
            pltpu.VMEM((rows, nodes, nodes), BF16),
            pltpu.VMEM((quarter, nodes, nodes), BF16),
            pltpu.VMEM((APPS, GROUPS, per, rows, nodes), BF16),
            pltpu.VMEM((rows * vectors, nodes), F32),
            pltpu.VMEM((rows + slots, vectors, nodes), BF16),
            pltpu.VMEM((slots * vectors, nodes), BF16),
            pltpu.VMEM((APPS, slots * vectors, nodes), BF16),
            pltpu.VMEM((rows * vectors, nodes), F32),
            pltpu.VMEM((rows * vectors, nodes), F32),
            pltpu.VMEM((slots * vectors, nodes), F32),
            pltpu.VMEM((APPS - 1, slots * vectors, nodes), F32),
            pltpu.VMEM((GROUPS, per, rows, nodes), F32),
            pltpu.VMEM((APPS - 1, 2, half, rows, nodes), F32),
            pltpu.VMEM((APPS - 1, 2, per, rows, nodes), F32),
            pltpu.VMEM((per, rows, nodes), F32),
            pltpu.VMEM((per, rows, nodes), F32),
            pltpu.VMEM((rows, rows + slots), BF16),
            pltpu.VMEM((curve * 8, 128), jnp.int32),
            pltpu.VMEM((curve * 8, 128), jnp.int32),
            pltpu.VMEM((8, max(rows, slots, 128)), jnp.int32),
            pltpu.SMEM((8, max(rows, slots, 128)), jnp.int32),
            pltpu.VMEM((GROUPS, 8, nodes), F32),
            pltpu.VMEM((2, GROUPS, 8, nodes), F32),
            pltpu.VMEM((3, 16, nodes), F32),
            pltpu.VMEM((3, curve * 16, nodes), F32),
            dma((2,)),
            dma((2,)),
            dma,
            dma((APPS, 4)),
            dma((APPS, 4)),
            dma((APPS, 2)),
            dma((APPS - 1, 2)),
            dma((APPS - 1, 6)),
            dma((APPS - 1, 6)),
            dma((2, 2, GROUPS)),
            dma((3, 2)),
        ],
        compiler_params=pltpu.CompilerParams(
            collective_id=0, has_side_effects=True, vmem_limit_bytes=60 * 1024 * 1024
        ),
    )(state, block_cols.reshape(rows, 1), block_cols.reshape(1, rows), blocks.reshape(rows, nodes, nodes), diag_blocks)


def solution(mesh):
    return jax.shard_map(
        body,
        mesh=mesh,
        in_specs=(
            P("band", "curve", None),
            P("curve", "band", None, None),
            P(("curve", "band"), None, None),
            P("curve", "band"),
        ),
        out_specs=P("band", "curve", None),
        check_vma=False,
    )
```

```python
import functools

import jax
import jax.numpy as jnp
from jax import lax
from jax.experimental import pallas as pl
from jax.experimental.pallas import tpu as pltpu
from jax.sharding import PartitionSpec as P

CAP = 2
TAYLOR = 16
APPS = 3
GROUPS = 4

epsilon = 1e-06
time_step = 0.5
quadratic = 1.0

F32 = jnp.float32
BF16 = jnp.bfloat16


def phi_weights(alpha_first, beta_first, alpha_second):
    term_one = jnp.ones_like(alpha_first)
    term_two = jnp.zeros_like(alpha_first)
    total_one, total_two = term_one, term_two
    for turn in range(1, TAYLOR):
        factor = time_step / (turn + 1.0)
        next_one = factor * (alpha_first * term_one + beta_first * term_two)
        next_two = factor * (beta_first * term_one + alpha_second * term_two)
        term_one, term_two = next_one, next_two
        total_one, total_two = total_one + next_one, total_two + next_two
    return total_one, total_two


def extents(curve):
    deep = curve // 8 if curve >= 16 else curve // 2
    return deep, curve // deep


def kernel(
    curve,
    state_ref,
    col_ref,
    row_ref,
    blocks_hbm,
    diag_hbm,
    out_ref,
    blocks,
    turned,
    diag,
    slabs,
    staging,
    pool,
    outbox,
    inbox,
    mirrored,
    forward,
    ret_out,
    ret_in,
    share,
    relay_in,
    sum_in,
    first,
    rest,
    onehot,
    ask_out,
    ask_in,
    index_vmem,
    index_smem,
    quad,
    band_in,
    total_out,
    total_mid,
    total_two,
    total_in,
    load_sem,
    ask_sem,
    index_sem,
    slab_send,
    slab_recv,
    gather_sem,
    return_sem,
    sum_send,
    sum_recv,
    band_sem,
    total_sem,
):
    per, rows, nodes = state_ref.shape
    vectors = per * GROUPS
    half = per // 2
    slots = curve * CAP
    quarter = diag.shape[0]
    me = lax.axis_index("curve")
    band = lax.axis_index("band")
    shift = rows.bit_length() - 1
    deep, broad = extents(curve)

    def other(step):
        return lax.rem(band + step, GROUPS)

    def peer(step):
        return lax.rem(me + step, curve)

    def load(chunk_ref, buffer, n):
        return pltpu.make_async_copy(chunk_ref, buffer, load_sem.at[n])

    load(blocks_hbm, blocks, 0).start()
    load(diag_hbm, diag, 1).start()

    barrier = pltpu.get_barrier_semaphore()

    @pl.loop(1, curve)
    def _(step):
        pl.semaphore_signal(barrier, inc=1, device_id={"curve": peer(step)})

    for step in range(1, GROUPS):
        pl.semaphore_signal(barrier, inc=1, device_id={"band": other(step)})

    own_col = lax.shift_right_logical(col_ref[...], shift)
    own_row = lax.shift_right_logical(row_ref[...], shift)
    tgt_row = row_ref[...] & (rows - 1)
    remote_row = own_row != me
    sub = lax.broadcasted_iota(jnp.int32, (rows, rows), 0)
    lane = lax.broadcasted_iota(jnp.int32, (rows, rows), 1)
    same = own_col == own_row
    rank_row = jnp.sum((same & (sub < lane)).astype(jnp.int32), axis=0, keepdims=True)
    rank_col = jnp.sum((same & (lane < sub)).astype(jnp.int32), axis=1, keepdims=True)
    bucket_col = jnp.where(own_col != me, own_col * CAP + rank_col, -1)
    pick_row = jnp.where(remote_row, rows + own_row * CAP + rank_row, tgt_row)
    padded = jnp.where(remote_row, own_row * 8 + rank_row, -1)
    place = lax.broadcasted_iota(jnp.int32, (curve * 8, rows), 0)
    wanted = jnp.sum(jnp.where(place == padded, tgt_row + 1, 0), axis=1, keepdims=True)
    ask_out[...] = jnp.broadcast_to(wanted, ask_out.shape)
    ask_in[pl.ds(pl.multiple_of(me * 8, 8), 8), :] = jnp.zeros((8, ask_in.shape[1]), jnp.int32)
    lane_slot = lax.broadcasted_iota(jnp.int32, (rows, slots), 1)
    source = lax.broadcasted_iota(jnp.int32, (rows, slots), 0)
    row_of = jnp.sum(jnp.where(bucket_col == lane_slot, source, 0), axis=0, keepdims=True)
    index_vmem[0:1, 0:rows] = jnp.clip(pick_row, 0, rows + slots - 1)
    index_vmem[1:2, 0:slots] = jnp.clip(row_of, 0, rows - 1)
    onehot[:, 0:rows] = ((tgt_row == sub) & ~remote_row).astype(F32).astype(BF16)

    pl.semaphore_wait(barrier, curve - 1 + GROUPS - 1)

    def ask_copy(target, own):
        return pltpu.make_async_remote_copy(
            src_ref=ask_out.at[pl.ds(pl.multiple_of(target * 8, 8), 8)],
            dst_ref=ask_in.at[pl.ds(pl.multiple_of(own * 8, 8), 8)],
            send_sem=ask_sem.at[0],
            recv_sem=ask_sem.at[1],
            device_id={"curve": target},
        )

    share_of = rows // curve

    def send_asked():
        def turn(r):
            turned[r] = blocks[r].T

        @pl.loop(1, curve)
        def _(step):
            ask_copy(peer(step), me).start()
            for k in range(share_of):
                turn(step * share_of + k)

        for k in range(share_of):
            turn(k)

    def wait_all(buffer, size, send, recv, wait_send):
        view = buffer.at[pl.ds(0, (curve - 1) * size)]
        copy = pltpu.make_async_remote_copy(
            src_ref=view, dst_ref=view, send_sem=send, recv_sem=recv, device_id={"curve": peer(1)}
        )
        if wait_send:
            copy.wait_send()
        else:
            copy.wait_recv()

    def take_asked():
        wait_all(ask_in, 8, ask_sem.at[0], ask_sem.at[1], False)
        place = lax.broadcasted_iota(jnp.int32, (curve * 8, slots), 0)
        slot = lax.broadcasted_iota(jnp.int32, (curve * 8, slots), 1)
        chosen = place == lax.shift_right_logical(slot, 1) * 8 + (slot & 1)
        asked = jnp.sum(jnp.where(chosen, ask_in[:, 0:slots], 0), axis=0, keepdims=True)
        index_vmem[2:3, 0:slots] = jnp.clip(asked - 1, 0, rows - 1)
        sub = lax.broadcasted_iota(jnp.int32, (rows, slots), 0)
        onehot[:, rows:] = (asked - 1 == sub).astype(F32).astype(BF16)
        copy = pltpu.make_async_copy(index_vmem, index_smem, index_sem)
        copy.start()
        copy.wait()
        wait_all(ask_out, 8, ask_sem.at[0], ask_sem.at[1], True)

    def slab_copy(app, src, dst, planes, step, n):
        return pltpu.make_async_remote_copy(
            src_ref=slabs.at[app, src, planes],
            dst_ref=slabs.at[app, dst, planes],
            send_sem=slab_send.at[app, n],
            recv_sem=slab_recv.at[app, n],
            device_id={"band": other(step)},
        )

    def interleave(app, group):
        for t in range(per):
            v = group * per + t
            staging[pl.ds(v, rows, stride=vectors), :] = slabs[app, group, t].astype(F32)

    low, high, every = pl.ds(0, half), pl.ds(half, half), pl.ds(0, per)

    def exchange_band(app, field, between=lambda: None):
        for t in range(per):
            slabs[app, 0, t] = field[t].astype(BF16)
        right = slab_copy(app, 0, 3, every, 1, 0)
        left = slab_copy(app, 0, 1, every, GROUPS - 1, 1)
        right.start()
        left.start()
        between()
        interleave(app, 0)
        right.wait_recv()
        on_right = slab_copy(app, 3, 2, low, 1, 2)
        on_right.start()
        left.wait_recv()
        on_left = slab_copy(app, 1, 2, high, GROUPS - 1, 3)
        on_left.start()
        interleave(app, 3)
        interleave(app, 1)
        on_right.wait_recv()
        on_left.wait_recv()
        interleave(app, 2)
        for copy in (right, left, on_right, on_left):
            copy.wait_send()

        @pl.loop(0, rows // 16)
        def _(n):
            piece = pl.ds(pl.multiple_of(n * 16 * vectors, 256), 16 * vectors)
            pool[pl.ds(pl.multiple_of(n * 16, 16), 16)] = (
                staging[piece, :].astype(BF16).reshape(16, vectors, nodes)
            )

    def tile(n):
        return pl.ds(pl.multiple_of(n * vectors, 16), vectors)

    wide = CAP * vectors

    def mirror(r):
        mirrored[tile(r), :] = jnp.dot(pool[r], blocks[r], preferred_element_type=F32)

    def send_gather(app):
        @pl.loop(1, curve)
        def _(step):
            target = peer(step)
            for k in range(CAP):
                n = target * CAP + k
                outbox[tile(n), :] = pool[index_smem[2, n]]
            if app < APPS - 1:
                for k in range(share_of):
                    mirror(step * share_of + k)
            pltpu.make_async_remote_copy(
                src_ref=outbox.at[pl.ds(pl.multiple_of(target * wide, wide), wide)],
                dst_ref=inbox.at[app, pl.ds(pl.multiple_of(me * wide, wide), wide)],
                send_sem=gather_sem.at[app, 0],
                recv_sem=gather_sem.at[app, 1],
                device_id={"curve": target},
            ).start()

        if app < APPS - 1:
            for k in range(share_of):
                mirror(k)

    def take_gather(app):
        wait_all(inbox.at[app], wide, gather_sem.at[app, 0], gather_sem.at[app, 1], False)

        @pl.loop(0, slots // 8)
        def _(n):
            piece = pl.ds(pl.multiple_of(n * 8 * vectors, 128), 8 * vectors)
            pool[pl.ds(rows + n * 8, 8)] = inbox[app, piece, :].reshape(8, vectors, nodes)

        wait_all(outbox, wide, gather_sem.at[app, 0], gather_sem.at[app, 1], True)

    def send_return(app):
        mine = pl.ds(pl.multiple_of(me * wide, wide), wide)
        ret_in[app, mine, :] = jnp.zeros((wide, nodes), F32)

        @pl.loop(1, curve)
        def _(step):
            target = peer(step)
            for k in range(CAP):
                n = target * CAP + k
                r = index_smem[1, n]
                ret_out[tile(n), :] = jnp.dot(pool[r], blocks[r], preferred_element_type=F32)
            pltpu.make_async_remote_copy(
                src_ref=ret_out.at[pl.ds(pl.multiple_of(target * wide, wide), wide)],
                dst_ref=ret_in.at[app, mine],
                send_sem=return_sem.at[app, 0],
                recv_sem=return_sem.at[app, 1],
                device_id={"curve": target},
            ).start()

    def multiply_forward(app):
        zeros = jnp.zeros((vectors, nodes), F32)

        def one(r, total):
            product = jnp.dot(pool[index_smem[0, r]], turned[r], preferred_element_type=F32)
            if app < APPS - 1:
                forward[tile(r), :] = product
            if app > 0:
                total = total + product * pool[r].astype(F32)
            return total

        total = lax.fori_loop(0, rows, one, zeros, unroll=min(rows, 32))

        def two(q, total):
            r = band * quarter + q
            left = pool[r]
            product = jnp.dot(left, diag[q], preferred_element_type=F32)
            if app < APPS - 1:
                forward[tile(r), :] += product
            if app > 0:
                total = total + product * left.astype(F32)
            return total

        return lax.fori_loop(0, quarter, two, 2.0 * total, unroll=min(quarter, 16))

    def split(value):
        upper = value.astype(BF16)
        return upper, (value - upper.astype(F32)).astype(BF16)

    def add_up(app, group, t):
        v = group * per + t
        here = mirrored[pl.ds(v, rows, stride=vectors), :]
        returned = ret_in[app, pl.ds(v, slots, stride=vectors), :]
        parts = jnp.concatenate(split(jnp.concatenate([here, returned], axis=0)), axis=1)
        both = jnp.dot(onehot[...], parts, preferred_element_type=F32)
        own = forward[pl.ds(v, rows, stride=vectors), :]
        share[group, t] = own + (both[:, 0:nodes] + both[:, nodes:])

    def sum_copy(app, src, dst, step, n):
        return pltpu.make_async_remote_copy(
            src_ref=src,
            dst_ref=dst,
            send_sem=sum_send.at[app, n],
            recv_sem=sum_recv.at[app, n],
            device_id={"band": other(step)},
        )

    def reduce_band(app, early=lambda: None, late=lambda: None):
        wait_all(ret_in.at[app], wide, return_sem.at[app, 0], return_sem.at[app, 1], False)
        up, down = 1, GROUPS - 1
        for t in range(half):
            add_up(app, 2, t)
        relay_up = sum_copy(app, share.at[2, low], relay_in.at[app, 0], up, 0)
        relay_up.start()
        for t in range(half, per):
            add_up(app, 2, t)
        relay_down = sum_copy(app, share.at[2, high], relay_in.at[app, 1], down, 1)
        relay_down.start()
        for t in range(half, per):
            add_up(app, 1, t)
        direct_up = sum_copy(app, share.at[1, high], sum_in.at[app, 0, high], up, 2)
        direct_up.start()
        for t in range(half):
            add_up(app, 3, t)
        direct_down = sum_copy(app, share.at[3, low], sum_in.at[app, 1, low], down, 3)
        direct_down.start()
        early()
        for t in range(half):
            add_up(app, 1, t)
        relay_up.wait_recv()
        share[1, 0:half] += relay_in[app, 0]
        last_up = sum_copy(app, share.at[1, low], sum_in.at[app, 0, low], up, 4)
        last_up.start()
        for t in range(half, per):
            add_up(app, 3, t)
        relay_down.wait_recv()
        share[3, half:per] += relay_in[app, 1]
        last_down = sum_copy(app, share.at[3, high], sum_in.at[app, 1, high], down, 5)
        last_down.start()
        late()
        for t in range(per):
            add_up(app, 0, t)
        copies = (relay_up, relay_down, direct_up, direct_down, last_up, last_down)
        for copy in copies[2:]:
            copy.wait_recv()
        for t in range(per):
            share[0, t] = share[0, t] + (sum_in[app, 0, t] + sum_in[app, 1, t])
        for copy in copies:
            copy.wait_send()
        wait_all(ret_out, wide, return_sem.at[app, 0], return_sem.at[app, 1], True)

    def send_quad(n, total):
        quad[...] = jnp.zeros_like(quad)
        for group in range(GROUPS):
            quad[group, 0:per, :] = total[group * per : (group + 1) * per, :]
        for step in range(1, GROUPS):
            pltpu.make_async_remote_copy(
                src_ref=quad.at[step],
                dst_ref=band_in.at[n, step],
                send_sem=band_sem.at[n, 0, step],
                recv_sem=band_sem.at[n, 1, step],
                device_id={"band": other(step)},
            ).start()

    def take_quad(n):
        total = quad[0]
        for step in range(1, GROUPS):
            copy = pltpu.make_async_remote_copy(
                src_ref=quad.at[step],
                dst_ref=band_in.at[n, step],
                send_sem=band_sem.at[n, 0, step],
                recv_sem=band_sem.at[n, 1, step],
                device_id={"band": other(step)},
            )
            copy.wait_recv()
            total = total + band_in[n, step]
            copy.wait_send()
        return total[0:per]

    def send_total(n, parts):
        total_out[n] = jnp.zeros_like(total_out[n])
        for k, part in enumerate(parts):
            total_out[n, k * per : (k + 1) * per, :] = part
        total_stage(n, 0)

    def total_peer(stage, step):
        if stage == 0:
            z = lax.rem(me, 2 * deep) // 2
            return me + 2 * (lax.rem(z + step, deep) - z)
        wide = (me // (2 * deep)) * 2 + lax.rem(me, 2)
        there = lax.rem(wide + step, broad)
        return (there // 2) * 2 * deep + me % (2 * deep) // 2 * 2 + lax.rem(there, 2)

    def total_buffers(n, stage):
        if stage == 0:
            return total_out.at[n], total_mid.at[n], deep, lax.rem(me, 2 * deep) // 2
        mine = (me // (2 * deep)) * 2 + lax.rem(me, 2)
        return total_two.at[n], total_in.at[n], broad, mine

    def total_stage(n, stage):
        source, target, count, slot = total_buffers(n, stage)
        mine = pl.ds(pl.multiple_of(slot * 16, 16), 16)
        target[mine, :] = source[...]
        for step in range(1, count):
            pltpu.make_async_remote_copy(
                src_ref=source,
                dst_ref=target.at[mine],
                send_sem=total_sem.at[n, stage, 0],
                recv_sem=total_sem.at[n, stage, 1],
                device_id={"curve": total_peer(stage, step)},
            ).start()

    def total_wait(n, stage):
        _, target, count, _ = total_buffers(n, stage)
        view = target.at[pl.ds(0, (count - 1) * 16)]
        copy = pltpu.make_async_remote_copy(
            src_ref=view,
            dst_ref=view,
            send_sem=total_sem.at[n, stage, 0],
            recv_sem=total_sem.at[n, stage, 1],
            device_id={"curve": total_peer(stage, 1)},
        )
        copy.wait_recv()
        total = jnp.sum(target[...].reshape(count, 16, nodes), axis=0)
        copy.wait_send()
        return total

    def pass_total(n):
        total_two[n] = total_wait(n, 0)
        total_stage(n, 1)

    def take_total(n):
        total = total_wait(n, 1)
        total = jnp.broadcast_to(jnp.sum(total, axis=1, keepdims=True), total.shape)
        return [total[k * per : (k + 1) * per] for k in range(4)]

    def over_rows(values):
        return jnp.concatenate([jnp.sum(value, axis=0, keepdims=True) for value in values], axis=0)

    def ask():
        load(blocks_hbm, blocks, 0).wait()
        load(diag_hbm, diag, 1).wait()
        send_asked()

    exchange_band(0, state_ref, ask)
    take_asked()
    send_gather(0)
    send_return(0)
    take_gather(0)
    multiply_forward(0)
    reduce_band(0)
    norms = []
    for t in range(per):
        field = state_ref[t]
        drive = share[0, t] + (quadratic * field * field - field * field * field)
        first[t] = drive
        norms.append(drive * drive)
    send_total(0, [over_rows(norms)])
    pass_total(0)
    norm_zero = take_total(0)[0]
    beta_zero = jnp.sqrt(norm_zero + epsilon)
    for t in range(per):
        first[t] = first[t] / beta_zero[t : t + 1]

    exchange_band(1, first)
    send_gather(1)
    send_return(1)
    take_gather(1)
    send_quad(0, multiply_forward(1))
    reduce_band(1, lambda: send_total(1, [take_quad(0)]), lambda: pass_total(1))
    alpha_first = take_total(1)[0]
    norms, along = [], []
    for t in range(per):
        value = share[0, t] - alpha_first[t : t + 1] * first[t]
        rest[t] = value
        norms.append(value * value)
        along.append(value * first[t])
    rest_norm = over_rows(norms)
    rest_along = over_rows(along)
    exchange_band(2, rest)
    send_gather(2)
    take_gather(2)
    send_quad(1, multiply_forward(2))
    send_total(2, [rest_norm, rest_along, take_quad(1)])
    pass_total(2)
    norm, dot, form, _ = take_total(2)
    squared = norm + epsilon
    beta_first = jnp.sqrt(squared)
    alpha_second = form / squared - dot
    weight_one, weight_two = phi_weights(alpha_first, beta_first, alpha_second)
    scale_one = time_step * beta_zero * weight_one
    scale_two = time_step * beta_zero * weight_two / beta_first
    for t in range(per):
        out_ref[t] = state_ref[t] + (
            scale_one[t : t + 1] * first[t] + scale_two[t : t + 1] * rest[t]
        )


def body(state, blocks, diag_blocks, block_cols):
    per, rows, nodes = state.shape
    curve = lax.axis_size("curve")
    vectors = per * GROUPS
    slots = curve * CAP
    half = per // 2
    quarter = diag_blocks.shape[0]
    deep, broad = extents(curve)
    dma = pltpu.SemaphoreType.DMA
    vmem = pl.BlockSpec(memory_space=pltpu.VMEM)
    anywhere = pl.BlockSpec(memory_space=pl.ANY)
    return pl.pallas_call(
        functools.partial(kernel, curve),
        out_shape=jax.ShapeDtypeStruct(state.shape, F32),
        in_specs=[vmem, vmem, vmem, anywhere, anywhere],
        out_specs=vmem,
        scratch_shapes=[
            pltpu.VMEM((rows, nodes, nodes), BF16),
            pltpu.VMEM((rows, nodes, nodes), BF16),
            pltpu.VMEM((quarter, nodes, nodes), BF16),
            pltpu.VMEM((APPS, GROUPS, per, rows, nodes), BF16),
            pltpu.VMEM((rows * vectors, nodes), F32),
            pltpu.VMEM((rows + slots, vectors, nodes), BF16),
            pltpu.VMEM((slots * vectors, nodes), BF16),
            pltpu.VMEM((APPS, slots * vectors, nodes), BF16),
            pltpu.VMEM((rows * vectors, nodes), F32),
            pltpu.VMEM((rows * vectors, nodes), F32),
            pltpu.VMEM((slots * vectors, nodes), F32),
            pltpu.VMEM((APPS - 1, slots * vectors, nodes), F32),
            pltpu.VMEM((GROUPS, per, rows, nodes), F32),
            pltpu.VMEM((APPS - 1, 2, half, rows, nodes), F32),
            pltpu.VMEM((APPS - 1, 2, per, rows, nodes), F32),
            pltpu.VMEM((per, rows, nodes), F32),
            pltpu.VMEM((per, rows, nodes), F32),
            pltpu.VMEM((rows, rows + slots), BF16),
            pltpu.VMEM((curve * 8, 128), jnp.int32),
            pltpu.VMEM((curve * 8, 128), jnp.int32),
            pltpu.VMEM((8, max(rows, slots, 128)), jnp.int32),
            pltpu.SMEM((8, max(rows, slots, 128)), jnp.int32),
            pltpu.VMEM((GROUPS, 8, nodes), F32),
            pltpu.VMEM((2, GROUPS, 8, nodes), F32),
            pltpu.VMEM((3, 16, nodes), F32),
            pltpu.VMEM((3, deep * 16, nodes), F32),
            pltpu.VMEM((3, 16, nodes), F32),
            pltpu.VMEM((3, broad * 16, nodes), F32),
            dma((2,)),
            dma((2,)),
            dma,
            dma((APPS, 4)),
            dma((APPS, 4)),
            dma((APPS, 2)),
            dma((APPS - 1, 2)),
            dma((APPS - 1, 6)),
            dma((APPS - 1, 6)),
            dma((2, 2, GROUPS)),
            dma((3, 2, 2)),
        ],
        compiler_params=pltpu.CompilerParams(
            collective_id=0, has_side_effects=True, vmem_limit_bytes=60 * 1024 * 1024
        ),
    )(state, block_cols.reshape(rows, 1), block_cols.reshape(1, rows), blocks.reshape(rows, nodes, nodes), diag_blocks)


def solution(mesh):
    return jax.shard_map(
        body,
        mesh=mesh,
        in_specs=(
            P("band", "curve", None),
            P("curve", "band", None, None),
            P(("curve", "band"), None, None),
            P("curve", "band"),
        ),
        out_specs=P("band", "curve", None),
        check_vma=False,
    )
```

```python
import functools

import jax
import jax.numpy as jnp
from jax import lax
from jax.experimental import pallas as pl
from jax.experimental.pallas import tpu as pltpu
from jax.sharding import PartitionSpec as P

CAP = 2
TAYLOR = 16
APPS = 3
GROUPS = 4

epsilon = 1e-06
time_step = 0.5
quadratic = 1.0

F32 = jnp.float32
BF16 = jnp.bfloat16


def phi_weights(alpha_first, beta_first, alpha_second):
    term_one = jnp.ones_like(alpha_first)
    term_two = jnp.zeros_like(alpha_first)
    total_one, total_two = term_one, term_two
    for turn in range(1, TAYLOR):
        factor = time_step / (turn + 1.0)
        next_one = factor * (alpha_first * term_one + beta_first * term_two)
        next_two = factor * (beta_first * term_one + alpha_second * term_two)
        term_one, term_two = next_one, next_two
        total_one, total_two = total_one + next_one, total_two + next_two
    return total_one, total_two


def extents(curve):
    deep = curve // 8 if curve >= 16 else curve // 2
    return deep, curve // deep


def kernel(
    curve,
    state_ref,
    col_ref,
    row_ref,
    blocks_hbm,
    diag_hbm,
    out_ref,
    blocks,
    turned,
    diag,
    slabs,
    staging,
    pool,
    outbox,
    inbox,
    mirrored,
    forward,
    ret_out,
    ret_in,
    ret_out_two,
    ret_in_two,
    share,
    relay_in,
    sum_in,
    first,
    rest,
    onehot,
    ask_out,
    ask_in,
    index_vmem,
    index_smem,
    quad,
    band_in,
    total_out,
    total_mid,
    total_two,
    total_in,
    load_sem,
    ask_sem,
    index_sem,
    slab_send,
    slab_recv,
    gather_sem,
    return_sem,
    sum_send,
    sum_recv,
    band_sem,
    total_sem,
):
    per, rows, nodes = state_ref.shape
    vectors = per * GROUPS
    half = per // 2
    slots = curve * CAP
    quarter = diag.shape[0]
    me = lax.axis_index("curve")
    band = lax.axis_index("band")
    shift = rows.bit_length() - 1
    deep, broad = extents(curve)

    def other(step):
        return lax.rem(band + step, GROUPS)

    def peer(step):
        return lax.rem(me + step, curve)

    def load(chunk_ref, buffer, n):
        return pltpu.make_async_copy(chunk_ref, buffer, load_sem.at[n])

    load(blocks_hbm, blocks, 0).start()
    load(diag_hbm, diag, 1).start()

    barrier = pltpu.get_barrier_semaphore()

    @pl.loop(1, curve)
    def _(step):
        pl.semaphore_signal(barrier, inc=1, device_id={"curve": peer(step)})

    for step in range(1, GROUPS):
        pl.semaphore_signal(barrier, inc=1, device_id={"band": other(step)})

    own_col = lax.shift_right_logical(col_ref[...], shift)
    own_row = lax.shift_right_logical(row_ref[...], shift)
    tgt_row = row_ref[...] & (rows - 1)
    remote_row = own_row != me
    sub = lax.broadcasted_iota(jnp.int32, (rows, rows), 0)
    lane = lax.broadcasted_iota(jnp.int32, (rows, rows), 1)
    same = own_col == own_row
    rank_row = jnp.sum((same & (sub < lane)).astype(jnp.int32), axis=0, keepdims=True)
    rank_col = jnp.sum((same & (lane < sub)).astype(jnp.int32), axis=1, keepdims=True)
    bucket_col = jnp.where(own_col != me, own_col * CAP + rank_col, -1)
    pick_row = jnp.where(remote_row, rows + own_row * CAP + rank_row, tgt_row)
    padded = jnp.where(remote_row, own_row * 8 + rank_row, -1)
    place = lax.broadcasted_iota(jnp.int32, (curve * 8, rows), 0)
    wanted = jnp.sum(jnp.where(place == padded, tgt_row + 1, 0), axis=1, keepdims=True)
    ask_out[...] = jnp.broadcast_to(wanted, ask_out.shape)
    ask_in[pl.ds(pl.multiple_of(me * 8, 8), 8), :] = jnp.zeros((8, ask_in.shape[1]), jnp.int32)
    lane_slot = lax.broadcasted_iota(jnp.int32, (rows, slots), 1)
    source = lax.broadcasted_iota(jnp.int32, (rows, slots), 0)
    row_of = jnp.sum(jnp.where(bucket_col == lane_slot, source, 0), axis=0, keepdims=True)
    index_vmem[0:1, 0:rows] = jnp.clip(pick_row, 0, rows + slots - 1)
    index_vmem[1:2, 0:slots] = jnp.clip(row_of, 0, rows - 1)
    onehot[:, 0:rows] = ((tgt_row == sub) & ~remote_row).astype(F32).astype(BF16)

    pl.semaphore_wait(barrier, curve - 1 + GROUPS - 1)

    def ask_copy(target, own):
        return pltpu.make_async_remote_copy(
            src_ref=ask_out.at[pl.ds(pl.multiple_of(target * 8, 8), 8)],
            dst_ref=ask_in.at[pl.ds(pl.multiple_of(own * 8, 8), 8)],
            send_sem=ask_sem.at[0],
            recv_sem=ask_sem.at[1],
            device_id={"curve": target},
        )

    share_of = rows // curve

    def send_asked():
        def turn(r):
            turned[r] = blocks[r].T

        @pl.loop(1, curve)
        def _(step):
            ask_copy(peer(step), me).start()
            for k in range(share_of):
                turn(step * share_of + k)

        for k in range(share_of):
            turn(k)

    def wait_all(buffer, size, send, recv, wait_send):
        view = buffer.at[pl.ds(0, (curve - 1) * size)]
        copy = pltpu.make_async_remote_copy(
            src_ref=view, dst_ref=view, send_sem=send, recv_sem=recv, device_id={"curve": peer(1)}
        )
        if wait_send:
            copy.wait_send()
        else:
            copy.wait_recv()

    def take_asked():
        wait_all(ask_in, 8, ask_sem.at[0], ask_sem.at[1], False)
        place = lax.broadcasted_iota(jnp.int32, (curve * 8, slots), 0)
        slot = lax.broadcasted_iota(jnp.int32, (curve * 8, slots), 1)
        chosen = place == lax.shift_right_logical(slot, 1) * 8 + (slot & 1)
        asked = jnp.sum(jnp.where(chosen, ask_in[:, 0:slots], 0), axis=0, keepdims=True)
        index_vmem[2:3, 0:slots] = jnp.clip(asked - 1, 0, rows - 1)
        sub = lax.broadcasted_iota(jnp.int32, (rows, slots), 0)
        onehot[:, rows:] = (asked - 1 == sub).astype(F32).astype(BF16)
        copy = pltpu.make_async_copy(index_vmem, index_smem, index_sem)
        copy.start()
        copy.wait()
        wait_all(ask_out, 8, ask_sem.at[0], ask_sem.at[1], True)

    def slab_copy(app, src, dst, planes, step, n):
        return pltpu.make_async_remote_copy(
            src_ref=slabs.at[app, src, planes],
            dst_ref=slabs.at[app, dst, planes],
            send_sem=slab_send.at[app, n],
            recv_sem=slab_recv.at[app, n],
            device_id={"band": other(step)},
        )

    def position(group, t):
        return (group * per + t - per - half) % vectors

    def interleave(app, group):
        for t in range(per):
            staging[pl.ds(position(group, t), rows, stride=vectors), :] = slabs[app, group, t].astype(F32)

    low, high, every = pl.ds(0, half), pl.ds(half, half), pl.ds(0, per)

    def exchange_band(app, field, between=lambda: None):
        for t in range(per):
            slabs[app, 0, t] = field[t].astype(BF16)
        right = slab_copy(app, 0, 3, every, 1, 0)
        left = slab_copy(app, 0, 1, every, GROUPS - 1, 1)
        right.start()
        left.start()
        between()
        interleave(app, 0)
        right.wait_recv()
        on_right = slab_copy(app, 3, 2, low, 1, 2)
        on_right.start()
        left.wait_recv()
        on_left = slab_copy(app, 1, 2, high, GROUPS - 1, 3)
        on_left.start()
        interleave(app, 3)
        interleave(app, 1)
        on_right.wait_recv()
        on_left.wait_recv()
        interleave(app, 2)
        for copy in (right, left, on_right, on_left):
            copy.wait_send()

        @pl.loop(0, rows // 16)
        def _(n):
            piece = pl.ds(pl.multiple_of(n * 16 * vectors, 256), 16 * vectors)
            pool[pl.ds(pl.multiple_of(n * 16, 16), 16)] = (
                staging[piece, :].astype(BF16).reshape(16, vectors, nodes)
            )

    def tile(n):
        return pl.ds(pl.multiple_of(n * vectors, 16), vectors)

    wide = CAP * vectors

    def mirror(r):
        mirrored[tile(r), :] = jnp.dot(pool[r], blocks[r], preferred_element_type=F32)

    def send_gather(app):
        @pl.loop(1, curve)
        def _(step):
            target = peer(step)
            for k in range(CAP):
                n = target * CAP + k
                outbox[tile(n), :] = pool[index_smem[2, n]]
            if app < APPS - 1:
                for k in range(share_of):
                    mirror(step * share_of + k)
            pltpu.make_async_remote_copy(
                src_ref=outbox.at[pl.ds(pl.multiple_of(target * wide, wide), wide)],
                dst_ref=inbox.at[app, pl.ds(pl.multiple_of(me * wide, wide), wide)],
                send_sem=gather_sem.at[app, 0],
                recv_sem=gather_sem.at[app, 1],
                device_id={"curve": target},
            ).start()

        if app < APPS - 1:
            for k in range(share_of):
                mirror(k)

    def take_gather(app):
        wait_all(inbox.at[app], wide, gather_sem.at[app, 0], gather_sem.at[app, 1], False)

        @pl.loop(0, slots // 8)
        def _(n):
            piece = pl.ds(pl.multiple_of(n * 8 * vectors, 128), 8 * vectors)
            pool[pl.ds(rows + n * 8, 8)] = inbox[app, piece, :].reshape(8, vectors, nodes)

        wait_all(outbox, wide, gather_sem.at[app, 0], gather_sem.at[app, 1], True)

    part_rows = vectors // 2
    pair = CAP * part_rows

    def return_buffers(app):
        return (ret_out, ret_in) if app == 0 else (ret_out_two, ret_in_two)

    def return_copy(app, part, target):
        source, arrived = return_buffers(app)
        return pltpu.make_async_remote_copy(
            src_ref=source.at[part, pl.ds(pl.multiple_of(target * pair, pair), pair)],
            dst_ref=arrived.at[part, pl.ds(pl.multiple_of(me * pair, pair), pair)],
            send_sem=return_sem.at[app, part, 0],
            recv_sem=return_sem.at[app, part, 1],
            device_id={"curve": target},
        )

    def send_return(app):
        source, arrived = return_buffers(app)
        mine = pl.ds(pl.multiple_of(me * pair, pair), pair)
        for part in range(2):
            arrived[part, mine, :] = jnp.zeros((pair, nodes), arrived.dtype)

        @pl.loop(1, curve)
        def _(step):
            target = peer(step)
            products = []
            for k in range(CAP):
                r = index_smem[1, target * CAP + k]
                products.append(jnp.dot(pool[r], blocks[r], preferred_element_type=F32))
            there = pl.ds(pl.multiple_of(target * pair, pair), pair)
            for part in range(2):
                own = [value[part * part_rows : (part + 1) * part_rows] for value in products]
                source[part, there, :] = jnp.concatenate(own, axis=0).astype(source.dtype)
            return_copy(app, 0, target).start()

        @pl.loop(1, curve)
        def _(step):
            return_copy(app, 1, peer(step)).start()

    def take_return(app, part):
        source, arrived = return_buffers(app)
        sems = (return_sem.at[app, part, 0], return_sem.at[app, part, 1])
        wait_all(arrived.at[part], pair, *sems, False)

    def end_return(app, part):
        source, _ = return_buffers(app)
        sems = (return_sem.at[app, part, 0], return_sem.at[app, part, 1])
        wait_all(source.at[part], pair, *sems, True)

    def multiply_forward(app):
        zeros = jnp.zeros((vectors, nodes), F32)

        def one(r, total):
            product = jnp.dot(pool[index_smem[0, r]], turned[r], preferred_element_type=F32)
            if app < APPS - 1:
                forward[tile(r), :] = product
            if app > 0:
                total = total + product * pool[r].astype(F32)
            return total

        total = lax.fori_loop(0, rows, one, zeros, unroll=min(rows, 32))

        def two(q, total):
            r = band * quarter + q
            left = pool[r]
            product = jnp.dot(left, diag[q], preferred_element_type=F32)
            if app < APPS - 1:
                forward[tile(r), :] += product
            if app > 0:
                total = total + product * left.astype(F32)
            return total

        return lax.fori_loop(0, quarter, two, 2.0 * total, unroll=min(quarter, 16))

    def split(value):
        upper = value.astype(BF16)
        return upper, (value - upper.astype(F32)).astype(BF16)

    def add_up(app, group, t):
        v = position(group, t)
        here = mirrored[pl.ds(v, rows, stride=vectors), :]
        arrived = return_buffers(app)[1]
        returned = arrived[v // part_rows, pl.ds(v % part_rows, slots, stride=part_rows), :]
        parts = jnp.concatenate(split(jnp.concatenate([here, returned], axis=0)), axis=1)
        both = jnp.dot(onehot[...], parts, preferred_element_type=F32)
        own = forward[pl.ds(v, rows, stride=vectors), :]
        share[group, t] = own + (both[:, 0:nodes] + both[:, nodes:])

    def sum_copy(app, src, dst, step, n):
        return pltpu.make_async_remote_copy(
            src_ref=src,
            dst_ref=dst,
            send_sem=sum_send.at[app, n],
            recv_sem=sum_recv.at[app, n],
            device_id={"band": other(step)},
        )

    def reduce_band(app, early=lambda: None, late=lambda: None):
        take_return(app, 0)
        up, down = 1, GROUPS - 1
        for t in range(half):
            add_up(app, 2, t)
        relay_up = sum_copy(app, share.at[2, low], relay_in.at[app, 0], up, 0)
        relay_up.start()
        for t in range(half, per):
            add_up(app, 2, t)
        relay_down = sum_copy(app, share.at[2, high], relay_in.at[app, 1], down, 1)
        relay_down.start()
        for t in range(half, per):
            add_up(app, 1, t)
        direct_up = sum_copy(app, share.at[1, high], sum_in.at[app, 0, high], up, 2)
        direct_up.start()
        for t in range(half):
            add_up(app, 3, t)
        direct_down = sum_copy(app, share.at[3, low], sum_in.at[app, 1, low], down, 3)
        direct_down.start()
        early()
        take_return(app, 1)
        for t in range(half):
            add_up(app, 1, t)
        relay_up.wait_recv()
        share[1, 0:half] += relay_in[app, 0]
        last_up = sum_copy(app, share.at[1, low], sum_in.at[app, 0, low], up, 4)
        last_up.start()
        for t in range(half, per):
            add_up(app, 3, t)
        relay_down.wait_recv()
        share[3, half:per] += relay_in[app, 1]
        last_down = sum_copy(app, share.at[3, high], sum_in.at[app, 1, high], down, 5)
        last_down.start()
        late()
        for t in range(per):
            add_up(app, 0, t)
        copies = (relay_up, relay_down, direct_up, direct_down, last_up, last_down)
        for copy in copies[2:]:
            copy.wait_recv()
        for t in range(per):
            share[0, t] = share[0, t] + (sum_in[app, 0, t] + sum_in[app, 1, t])
        for copy in copies:
            copy.wait_send()
        end_return(app, 0)
        end_return(app, 1)

    def send_quad(n, total):
        quad[...] = jnp.zeros_like(quad)
        for group in range(GROUPS):
            for t in range(0, per, half):
                v = position(group, t)
                quad[group, t : t + half, :] = total[v : v + half, :]
        for step in range(1, GROUPS):
            pltpu.make_async_remote_copy(
                src_ref=quad.at[step],
                dst_ref=band_in.at[n, step],
                send_sem=band_sem.at[n, 0, step],
                recv_sem=band_sem.at[n, 1, step],
                device_id={"band": other(step)},
            ).start()

    def take_quad(n):
        total = quad[0]
        for step in range(1, GROUPS):
            copy = pltpu.make_async_remote_copy(
                src_ref=quad.at[step],
                dst_ref=band_in.at[n, step],
                send_sem=band_sem.at[n, 0, step],
                recv_sem=band_sem.at[n, 1, step],
                device_id={"band": other(step)},
            )
            copy.wait_recv()
            total = total + band_in[n, step]
            copy.wait_send()
        return total[0:per]

    def send_total(n, parts):
        total_out[n] = jnp.zeros_like(total_out[n])
        for k, part in enumerate(parts):
            total_out[n, k * per : (k + 1) * per, :] = part
        total_stage(n, 0)

    def total_peer(stage, step):
        if stage == 0:
            z = lax.rem(me, 2 * deep) // 2
            return me + 2 * (lax.rem(z + step, deep) - z)
        wide = (me // (2 * deep)) * 2 + lax.rem(me, 2)
        there = lax.rem(wide + step, broad)
        return (there // 2) * 2 * deep + me % (2 * deep) // 2 * 2 + lax.rem(there, 2)

    def total_buffers(n, stage):
        if stage == 0:
            return total_out.at[n], total_mid.at[n], deep, lax.rem(me, 2 * deep) // 2
        mine = (me // (2 * deep)) * 2 + lax.rem(me, 2)
        return total_two.at[n], total_in.at[n], broad, mine

    def total_stage(n, stage):
        source, target, count, slot = total_buffers(n, stage)
        mine = pl.ds(pl.multiple_of(slot * 16, 16), 16)
        target[mine, :] = source[...]
        for step in range(1, count):
            pltpu.make_async_remote_copy(
                src_ref=source,
                dst_ref=target.at[mine],
                send_sem=total_sem.at[n, stage, 0],
                recv_sem=total_sem.at[n, stage, 1],
                device_id={"curve": total_peer(stage, step)},
            ).start()

    def total_wait(n, stage):
        _, target, count, _ = total_buffers(n, stage)
        view = target.at[pl.ds(0, (count - 1) * 16)]
        copy = pltpu.make_async_remote_copy(
            src_ref=view,
            dst_ref=view,
            send_sem=total_sem.at[n, stage, 0],
            recv_sem=total_sem.at[n, stage, 1],
            device_id={"curve": total_peer(stage, 1)},
        )
        copy.wait_recv()
        total = jnp.sum(target[...].reshape(count, 16, nodes), axis=0)
        copy.wait_send()
        return total

    def pass_total(n):
        total_two[n] = total_wait(n, 0)
        total_stage(n, 1)

    def take_total(n):
        total = total_wait(n, 1)
        total = jnp.broadcast_to(jnp.sum(total, axis=1, keepdims=True), total.shape)
        return [total[k * per : (k + 1) * per] for k in range(4)]

    def over_rows(values):
        return jnp.concatenate([jnp.sum(value, axis=0, keepdims=True) for value in values], axis=0)

    def ask():
        load(blocks_hbm, blocks, 0).wait()
        load(diag_hbm, diag, 1).wait()
        send_asked()

    exchange_band(0, state_ref, ask)
    take_asked()
    send_gather(0)
    send_return(0)
    take_gather(0)
    multiply_forward(0)
    reduce_band(0)
    norms = []
    for t in range(per):
        field = state_ref[t]
        drive = share[0, t] + (quadratic * field * field - field * field * field)
        first[t] = drive
        norms.append(drive * drive)
    send_total(0, [over_rows(norms)])
    pass_total(0)
    norm_zero = take_total(0)[0]
    beta_zero = jnp.sqrt(norm_zero + epsilon)
    for t in range(per):
        first[t] = first[t] / beta_zero[t : t + 1]

    exchange_band(1, first)
    send_gather(1)
    send_return(1)
    take_gather(1)
    send_quad(0, multiply_forward(1))
    reduce_band(1, lambda: send_total(1, [take_quad(0)]), lambda: pass_total(1))
    alpha_first = take_total(1)[0]
    norms, along = [], []
    for t in range(per):
        value = share[0, t] - alpha_first[t : t + 1] * first[t]
        rest[t] = value
        norms.append(value * value)
        along.append(value * first[t])
    rest_norm = over_rows(norms)
    rest_along = over_rows(along)
    exchange_band(2, rest)
    send_gather(2)
    take_gather(2)
    send_quad(1, multiply_forward(2))
    send_total(2, [rest_norm, rest_along, take_quad(1)])
    pass_total(2)
    norm, dot, form, _ = take_total(2)
    squared = norm + epsilon
    beta_first = jnp.sqrt(squared)
    alpha_second = form / squared - dot
    weight_one, weight_two = phi_weights(alpha_first, beta_first, alpha_second)
    scale_one = time_step * beta_zero * weight_one
    scale_two = time_step * beta_zero * weight_two / beta_first
    for t in range(per):
        out_ref[t] = state_ref[t] + (
            scale_one[t : t + 1] * first[t] + scale_two[t : t + 1] * rest[t]
        )


def body(state, blocks, diag_blocks, block_cols):
    per, rows, nodes = state.shape
    curve = lax.axis_size("curve")
    vectors = per * GROUPS
    slots = curve * CAP
    half = per // 2
    quarter = diag_blocks.shape[0]
    deep, broad = extents(curve)
    dma = pltpu.SemaphoreType.DMA
    vmem = pl.BlockSpec(memory_space=pltpu.VMEM)
    anywhere = pl.BlockSpec(memory_space=pl.ANY)
    return pl.pallas_call(
        functools.partial(kernel, curve),
        out_shape=jax.ShapeDtypeStruct(state.shape, F32),
        in_specs=[vmem, vmem, vmem, anywhere, anywhere],
        out_specs=vmem,
        scratch_shapes=[
            pltpu.VMEM((rows, nodes, nodes), BF16),
            pltpu.VMEM((rows, nodes, nodes), BF16),
            pltpu.VMEM((quarter, nodes, nodes), BF16),
            pltpu.VMEM((APPS, GROUPS, per, rows, nodes), BF16),
            pltpu.VMEM((rows * vectors, nodes), F32),
            pltpu.VMEM((rows + slots, vectors, nodes), BF16),
            pltpu.VMEM((slots * vectors, nodes), BF16),
            pltpu.VMEM((APPS, slots * vectors, nodes), BF16),
            pltpu.VMEM((rows * vectors, nodes), F32),
            pltpu.VMEM((rows * vectors, nodes), F32),
            pltpu.VMEM((2, slots * vectors // 2, nodes), F32),
            pltpu.VMEM((2, slots * vectors // 2, nodes), F32),
            pltpu.VMEM((2, slots * vectors // 2, nodes), F32),
            pltpu.VMEM((2, slots * vectors // 2, nodes), F32),
            pltpu.VMEM((GROUPS, per, rows, nodes), F32),
            pltpu.VMEM((APPS - 1, 2, half, rows, nodes), F32),
            pltpu.VMEM((APPS - 1, 2, per, rows, nodes), F32),
            pltpu.VMEM((per, rows, nodes), F32),
            pltpu.VMEM((per, rows, nodes), F32),
            pltpu.VMEM((rows, rows + slots), BF16),
            pltpu.VMEM((curve * 8, 128), jnp.int32),
            pltpu.VMEM((curve * 8, 128), jnp.int32),
            pltpu.VMEM((8, max(rows, slots, 128)), jnp.int32),
            pltpu.SMEM((8, max(rows, slots, 128)), jnp.int32),
            pltpu.VMEM((GROUPS, 8, nodes), F32),
            pltpu.VMEM((2, GROUPS, 8, nodes), F32),
            pltpu.VMEM((3, 16, nodes), F32),
            pltpu.VMEM((3, deep * 16, nodes), F32),
            pltpu.VMEM((3, 16, nodes), F32),
            pltpu.VMEM((3, broad * 16, nodes), F32),
            dma((2,)),
            dma((2,)),
            dma,
            dma((APPS, 4)),
            dma((APPS, 4)),
            dma((APPS, 2)),
            dma((APPS - 1, 2, 2)),
            dma((APPS - 1, 6)),
            dma((APPS - 1, 6)),
            dma((2, 2, GROUPS)),
            dma((3, 2, 2)),
        ],
        compiler_params=pltpu.CompilerParams(
            collective_id=0, has_side_effects=True, vmem_limit_bytes=60 * 1024 * 1024
        ),
    )(state, block_cols.reshape(rows, 1), block_cols.reshape(1, rows), blocks.reshape(rows, nodes, nodes), diag_blocks)


def solution(mesh):
    return jax.shard_map(
        body,
        mesh=mesh,
        in_specs=(
            P("band", "curve", None),
            P("curve", "band", None, None),
            P(("curve", "band"), None, None),
            P("curve", "band"),
        ),
        out_specs=P("band", "curve", None),
        check_vma=False,
    )
```
